32 devices in a mesh: section: 2 (over x), tensor: 16 (over z, y, core).
Axes of the slice: x: 2, y: 2, z: 4, core: 2. Of those that a mesh axis runs over, the one named last changes fastest.
Arguments:
- patches: bfloat16 [128, 1280], P(('section', 'tensor')), may hold values from -6 to 6
- intermediate: bfloat16 [128, 6400], P(('section', 'tensor')), may hold values from -6 to 6
- fc1_weight: bfloat16 [1280, 5120], P(None, 'tensor'), may hold values from -0.15625 to 0.15625
- fc2_weight: bfloat16 [5120, 1280], P('tensor'), may hold values from -0.078125 to 0.078125
- projector: bfloat16 [7680, 8192], P(None, 'tensor'), may hold values from -0.0625 to 0.0625
- text: bfloat16 [2, 256, 8192], P('section', None, 'tensor'), may hold values from -6 to 6
- query_weight: bfloat16 [2, 8192, 8192], P('section', None, 'tensor'), may hold values from -0.0625 to 0.0625
- kv_weight: bfloat16 [2, 8192, 2048], P('section', 'tensor'), may hold values from -0.0625 to 0.0625
- query_gain: float32 [2, 128], P('section')
- key_gain: float32 [2, 128], P('section')
- out_weight: bfloat16 [2, 8192, 8192], P('section', 'tensor'), may hold values from -0.09375 to 0.09375
- attn_gate: float32 [2], P('section'), may hold values from 0.4 to 1.4
- tile_list: int32 [2, 4, 4], P('section'), may hold values from 0 to 1
- list_count: int32 [2, 4], P('section'), may hold values from 1 to 4, as said below
Outputs:
- mixed: bfloat16 [2, 256, 8192], P('section', None, 'tensor')
The draws below stay inside these ranges and needn't reach their ends.
Inputs may be any that keep to these rules, and one draw needn't show every extreme that they name: `list_count`: some block has 4 used slots and some has one; tiles may repeat within a list.
All inputs are finite; a program needn't handle non-finite values.
Results may differ from the reference program's by a relative error of at most 0.017.
The reference program's roundings to bfloat16 on the way count: a program that leaves them out, or rounds other values in their place, can miss the bound.
Values may be sent and summed in bfloat16 or wider, within the bound.
A program may use at most 128 MiB of HBM per device.

```python
import jax
import jax.numpy as jnp
from jax import lax

DV = 1280
FFV = 5120
D = 8192
HEADS = 64
KV_HEADS = 8
HD = 128
TXT = 256
TILE_ROWS = 64
TBLOCK = 64
LIST = 4
INTER_W = 6400
KVW = 1024
SECTIONS = 2
IMG_ROWS = 128
TILES = 2
BLOCKS = 4


def draw_query_gain(key, part):
    key = jax.random.fold_in(key, 11)
    return jax.random.uniform(key, (SECTIONS, HD), jnp.float32, 1.5, 3.0)


def draw_key_gain(key, part):
    key = jax.random.fold_in(key, 23)
    return jax.random.uniform(key, (SECTIONS, HD), jnp.float32, 1.5, 3.0)


def draw_list_count(key, part):
    key = jax.random.fold_in(key, 37)
    key = jax.random.fold_in(key, part)
    counts = jax.random.randint(key, (SECTIONS, BLOCKS), 1, LIST + 1).astype(jnp.int32)
    counts = counts.at[:, 0].set(LIST)
    return counts.at[:, 1].set(1)


def touch_ends(values, stream_key, low, top_value):
    longest = values.shape.index(max(values.shape))
    spots = []
    for shift in (0, 1):
        where = [jax.random.randint(jax.random.fold_in(stream_key, axis), (), 0, length) for axis, length in enumerate(values.shape)]
        where[longest] = (where[longest] + shift) % values.shape[longest]
        spots.append(tuple(where))
    return values.at[spots[0]].set(low).at[spots[1]].set(top_value)


def with_spikes(values, own_key, source, target, parts, factor):
    owner, partner = [(jnp.arange(values.shape[axis_at]) // (values.shape[axis_at] // parts)).reshape([-1 if axis == axis_at else 1 for axis in range(values.ndim)]) for axis_at in (source, target)]
    chosen = jax.random.permutation(own_key, parts)[partner]
    strong = (owner == chosen) | (owner == (partner + parts // 2) % parts)
    return jnp.where(strong, factor * values, values)


def block_scale(rng, extent, cuts, low, high):
    def one(axis_at, shards_of):
        steps = jax.random.uniform(jax.random.fold_in(jax.random.fold_in(rng, 6), axis_at), (shards_of,), jnp.float32, low / len(cuts), high / len(cuts))
        return jnp.repeat(jnp.exp(steps), extent[axis_at] // shards_of).reshape((-1,) + (1,) * (len(extent) - axis_at - 1))

    level = one(*cuts[0])
    for cut in cuts[1:]:
        level = level * one(*cut)
    return level


def centred(rng, extent, width, limit, shards=(), kind=jnp.bfloat16):
    level = block_scale(rng, extent, shards, -0.22, 0.18) if shards else 1.0
    result = jax.random.normal(rng, extent, jnp.float32) * width * level
    return jnp.minimum(jnp.maximum(result, -limit), limit).astype(kind)


def gaussian_with(rng, dims, width, most, split, heavy, kind=jnp.bfloat16):
    entries = width * jax.random.normal(rng, dims, jnp.float32)
    if split:
        entries = entries * block_scale(rng, dims, split, -0.22, 0.18)
    return jnp.clip(with_spikes(entries, jax.random.fold_in(rng, 3), *heavy), -most, most).astype(kind)


def setup_inputs(seed: int = 0) -> dict:
    seeds = jax.random.split(jax.random.key(seed), 15)
    patches = centred(seeds[0], (IMG_ROWS, DV), 1.0, 6.0, ((0, 32),))
    intermediate = centred(seeds[1], (IMG_ROWS, INTER_W), 1.0, 6.0, ((0, 32),))
    fc1_weight = centred(seeds[2], (DV, FFV), DV ** -0.5, 0.15625, ((1, 16),))
    fc2_weight = centred(seeds[3], (FFV, DV), FFV ** -0.5, 0.078125, ((0, 16),))
    projector = centred(seeds[4], (6 * DV, D), (6 * DV) ** -0.5, 0.0625, ((1, 16),))
    text = centred(seeds[5], (SECTIONS, TXT, D), 1.0, 6.0, ((0, 2), (2, 16)))
    query_weight = centred(seeds[6], (SECTIONS, D, D), D ** -0.5, 0.0625, ((0, 2), (2, 16)))
    kv_weight = centred(seeds[7], (SECTIONS, D, 2 * KVW), D ** -0.5, 0.0625, ((0, 2), (1, 16)))
    query_gain = draw_query_gain(jax.random.fold_in(seeds[14], 71), 0)
    key_gain = draw_key_gain(jax.random.fold_in(seeds[14], 71), 0)
    out_weight = gaussian_with(seeds[10], (SECTIONS, D, D), D ** -0.5, 0.09375, ((0, 2), (1, 16)), (1, 2, 16, 2.0))
    attn_gate = jnp.clip(0.4 + 1 * jax.random.uniform(seeds[11], (SECTIONS,), jnp.float32) ** block_scale(seeds[11], (SECTIONS,), ((0, 2),), -0.2, 0.2), 0.4, 1.4)
    tile_list = touch_ends(jax.random.randint(seeds[12], (SECTIONS, BLOCKS, LIST), 0, TILES), jax.random.fold_in(seeds[12], 1), 0, TILES - 1).astype(jnp.int32)
    list_count = draw_list_count(jax.random.fold_in(seeds[14], 71), 0)
    return {"patches": patches, "intermediate": intermediate, "fc1_weight": fc1_weight, "fc2_weight": fc2_weight, "projector": projector, "text": text, "query_weight": query_weight, "kv_weight": kv_weight, "query_gain": query_gain, "key_gain": key_gain, "out_weight": out_weight, "attn_gate": attn_gate, "tile_list": tile_list, "list_count": list_count}


def layer_norm(values):
    center = values - lax.optimization_barrier(jnp.mean(values, axis=-1, keepdims=True))
    spread = lax.optimization_barrier(jnp.mean(center * center, axis=-1, keepdims=True))
    return center * lax.rsqrt(spread + 1e-06)

def rms_scale(values, gain):
    return values * lax.rsqrt(lax.optimization_barrier(jnp.mean(values * values, axis=-1, keepdims=True)) + 1e-05) * gain

def visible_rows(tiles, counts):
    slots = jnp.arange(LIST, dtype=jnp.int32)
    used = slots[None, :] < counts[:, None]
    targets = jnp.arange(TILES, dtype=jnp.int32)
    hits = (tiles[:, :, None] == targets[None, None, :]) & used[:, :, None]
    allowed = jnp.any(hits, axis=1)
    key_ok = jnp.repeat(allowed, TILE_ROWS, axis=1)
    return jnp.repeat(key_ok, TBLOCK, axis=0)

def reference(patches, intermediate, fc1_weight, fc2_weight, projector, text, query_weight, kv_weight, query_gain, key_gain, out_weight, attn_gate, tile_list, list_count):
    states = patches.astype(jnp.float32)
    normed = layer_norm(states).astype(jnp.bfloat16)
    hidden = jax.nn.gelu(jnp.dot(normed, fc1_weight, preferred_element_type=jnp.float32), approximate=False).astype(jnp.bfloat16)
    encoded = (states + jnp.dot(hidden, fc2_weight, preferred_element_type=jnp.float32)).astype(jnp.bfloat16)
    features = jnp.concatenate([encoded, intermediate], axis=1)
    image = jnp.dot(features, projector, preferred_element_type=jnp.float32).astype(jnp.bfloat16)
    group = HEADS // KV_HEADS
    results = []
    for section in range(SECTIONS):
        kv = jnp.dot(image, kv_weight[section], preferred_element_type=jnp.float32).astype(jnp.bfloat16)
        keys = kv[:, :KVW].astype(jnp.float32).reshape(IMG_ROWS, KV_HEADS, HD)
        values = kv[:, KVW:].reshape(IMG_ROWS, KV_HEADS, HD)
        key_normed = rms_scale(keys, key_gain[section]).astype(jnp.bfloat16)
        query = jnp.dot(text[section], query_weight[section], preferred_element_type=jnp.float32).reshape(TXT, HEADS, HD)
        query_normed = rms_scale(query, query_gain[section]).astype(jnp.bfloat16)
        key_heads = jnp.repeat(key_normed, group, axis=1).astype(jnp.float32)
        value_heads = jnp.repeat(values, group, axis=1).astype(jnp.float32)
        scores = jnp.einsum('thd,khd->htk', query_normed.astype(jnp.float32), key_heads) * (1.0 / HD ** 0.5)
        row_ok = visible_rows(tile_list[section], list_count[section])
        scores = jnp.where(row_ok[None], scores, -1e+30)
        top = lax.optimization_barrier(jnp.max(scores, axis=-1, keepdims=True))
        weights = jnp.exp(scores - top)
        probs = (weights / lax.optimization_barrier(jnp.sum(weights, axis=-1, keepdims=True))).astype(jnp.bfloat16)
        attended = jnp.einsum('htk,khd->thd', probs.astype(jnp.float32), value_heads).astype(jnp.bfloat16).reshape(TXT, D)
        branch = jnp.dot(attended, out_weight[section], preferred_element_type=jnp.float32)
        results.append((text[section].astype(jnp.float32) + jnp.tanh(attn_gate[section]) * branch).astype(jnp.bfloat16))
    return jnp.stack(results)
```

```python
import functools

import jax
import jax.numpy as jnp
from jax import lax
from jax.experimental import pallas as pl
from jax.experimental.pallas import tpu as pltpu
from jax.sharding import PartitionSpec as P

HEADS = 64
KV_HEADS = 8
HD = 128
TILE_ROWS = 64
TBLOCK = 64
F32 = jnp.float32
BF16 = jnp.bfloat16


def dot(a, b):
    return jnp.dot(a, b, preferred_element_type=F32)


def remote(src, dst, send, recv, **axes):
    return pltpu.make_async_remote_copy(
        src_ref=src,
        dst_ref=dst,
        send_sem=send,
        recv_sem=recv,
        device_id=axes,
        device_id_type=pl.DeviceIdType.MESH,
    )


def rms_scale(values, gain):
    return values * lax.rsqrt(jnp.mean(values * values, axis=-1, keepdims=True) + 1e-05) * gain


def each(first, last, body):
    def step(i, carry):
        body(i)
        return carry

    lax.fori_loop(first, last, step, 0)


def kernel(
    T,
    patches,
    inter,
    qgain,
    kgain,
    gate,
    tiles,
    counts,
    text,
    fc1_hbm,
    fc2_hbm,
    proj_hbm,
    qw_hbm,
    kvw_hbm,
    ow_hbm,
    out,
    fc1,
    fc2,
    proj,
    qw,
    kvw,
    ow,
    xr,
    xs,
    part,
    partr,
    er,
    ir,
    feats,
    img,
    tall,
    query,
    kvp,
    kcr,
    kzr,
    kvh,
    mask,
    att,
    ocs,
    ocr,
    own,
    oys,
    oyr,
    ozs,
    ozr,
    loc,
    xsem,
    rsem,
    esem,
    tz,
    ty,
    tc,
    iz,
    iy,
    ic,
    msem,
    kc,
    kz,
    kg,
    oc,
    oy,
    oz,
):
    A = T // 4
    J = T // 2
    G = T // KV_HEADS
    me = lax.axis_index("tensor")
    sec = lax.axis_index("section")
    z = me // 4
    y = (me // 2) % 2
    c = me % 2
    mj = me // 2
    pair = me + 1 - 2 * c
    across = me + 2 - 4 * y
    rows = patches.shape[0]
    group = T * rows
    dv = patches.shape[1]
    txt = tall.shape[1]
    width = tall.shape[2]
    hl = width // HD

    barrier = pltpu.get_barrier_semaphore()

    def greet(p):
        pl.semaphore_signal(
            barrier,
            inc=1,
            device_id={"tensor": (me + p) % T},
            device_id_type=pl.DeviceIdType.MESH,
        )

    each(1, T, greet)
    pl.semaphore_signal(
        barrier, inc=1, device_id={"section": 1 - sec}, device_id_type=pl.DeviceIdType.MESH
    )
    locals_ = [
        pltpu.make_async_copy(src, dst, loc.at[i])
        for i, (src, dst) in enumerate(
            (
                (text, tall.at[me]),
                (fc1_hbm, fc1),
                (fc2_hbm, fc2),
                (proj_hbm, proj),
                (kvw_hbm, kvw),
                (qw_hbm, qw),
                (ow_hbm, ow),
            )
        )
    ]
    for copy in locals_:
        copy.start()
    xr[me] = patches[...]
    ir[me] = inter[...]
    pl.semaphore_wait(barrier, T)

    def spread(buf, sem, p):
        return remote(
            buf.at[me], buf.at[me], sem.at[0, p], sem.at[1, me], tensor=(me + p) % T
        )

    def spread_in(buf, sem, p):
        src = (me + p) % T
        return remote(buf.at[src], buf.at[src], sem.at[0, p], sem.at[1, src], tensor=src)

    def part_out(p):
        to = (me + p) % T
        return remote(part.at[to], partr.at[me], rsem.at[0, p], rsem.at[1, me], tensor=to)

    def part_in(p):
        src = (me + p) % T
        return remote(part.at[src], partr.at[src], rsem.at[0, p], rsem.at[1, src], tensor=src)

    def line(buf, sem, p):
        to = ((z + p) % A) * 4 + y * 2 + c
        return remote(buf.at[me], buf.at[me], sem.at[0, p], sem.at[1, z], tensor=to)

    def line_in(buf, sem, p):
        zs = (z + p) % A
        src = zs * 4 + y * 2 + c
        return remote(buf.at[src], buf.at[src], sem.at[0, p], sem.at[1, zs], tensor=src)

    def cross(buf, sem, zs):
        b = zs * 4 + y * 2 + c
        return remote(buf.at[b], buf.at[b], sem.at[0, zs], sem.at[1, zs], tensor=across)

    def cross_in(buf, sem, zs):
        b = zs * 4 + (1 - y) * 2 + c
        return remote(buf.at[b], buf.at[b], sem.at[0, zs], sem.at[1, zs], tensor=across)

    def core(buf, sem, j):
        b = j * 2 + c
        return remote(buf.at[b], buf.at[b], sem.at[0, j], sem.at[1, j], tensor=pair)

    def core_in(buf, sem, j):
        b = j * 2 + 1 - c
        return remote(buf.at[b], buf.at[b], sem.at[0, j], sem.at[1, j], tensor=pair)

    def begin(buf, lz, ly, lc):
        each(1, A, lambda p: line(buf, lz, p).start())
        cross(buf, ly, z).start()
        core(buf, lc, mj).start()

    def pass_line(buf, lz, ly, lc):
        def body(p):
            zs = (z + p) % A
            line_in(buf, lz, p).wait_recv()
            cross(buf, ly, zs).start()
            core(buf, lc, zs * 2 + y).start()

        each(1, A, body)

    def pass_cross(buf, ly, lc):
        def body(p):
            zs = (z + p) % A
            cross_in(buf, ly, zs).wait_recv()
            core(buf, lc, zs * 2 + 1 - y).start()

        each(0, A, body)

    each(1, T, lambda p: spread(xr, xsem, p).start())
    begin(ir, iz, iy, ic)
    locals_[0].wait()
    begin(tall, tz, ty, tc)

    total = mask.shape[1]
    tile_of = lax.broadcasted_iota(jnp.int32, (TBLOCK, total), 1) // TILE_ROWS
    for b in range(tiles.shape[0]):
        seen = jnp.zeros((TBLOCK, total), F32)
        for j in range(tiles.shape[1]):
            listed = (tile_of == tiles[b : b + 1, j : j + 1]) & (counts[b : b + 1, :] > j)
            seen = jnp.where(listed, 1.0, seen)
        mask[b * TBLOCK : (b + 1) * TBLOCK, :] = seen

    each(1, T, lambda p: spread_in(xr, xsem, p).wait_recv())
    for i in range(T):
        xs[i * rows : (i + 1) * rows, :] = xr[i].astype(F32)
    states = xs[...]
    center = states - jnp.mean(states, axis=-1, keepdims=True)
    spread_sq = jnp.mean(center * center, axis=-1, keepdims=True)
    normed = (center * lax.rsqrt(spread_sq + 1e-06)).astype(BF16)
    locals_[1].wait()
    pre = dot(normed, fc1[...])
    hidden = (0.5 * pre * (1.0 + lax.erf(pre * (0.5**0.5)))).astype(BF16)
    locals_[2].wait()
    partial_value = dot(hidden, fc2[...])
    for i in range(T):
        part[i] = partial_value[i * rows : (i + 1) * rows, :]
    each(1, T, lambda p: part_out(p).start())
    pass_line(ir, iz, iy, ic)
    each(1, T, lambda p: part_in(p).wait_recv())
    total_value = lax.fori_loop(
        1, T, lambda p, acc: acc + partr[(me + p) % T], part[me]
    )
    er[me] = (patches[...].astype(F32) + total_value).astype(BF16)
    each(1, T, lambda p: spread(er, esem, p).start())
    pass_cross(ir, iy, ic)
    pass_line(tall, tz, ty, tc)

    each(0, J, lambda j: core_in(ir, ic, j).wait_recv())
    for i in range(T):
        xs[i * rows : (i + 1) * rows, :] = xr[i].astype(F32)
        feats[i * rows : (i + 1) * rows, :] = ir[i].astype(F32)
    locals_[3].wait()
    image = jnp.zeros((group, width), F32)
    chunks = inter.shape[1] // dv
    for k in range(chunks):
        image += dot(
            feats[:, k * dv : (k + 1) * dv].astype(BF16), proj[(k + 1) * dv : (k + 2) * dv, :]
        )
    each(1, T, lambda p: spread_in(er, esem, p).wait_recv())
    for i in range(T):
        xs[i * rows : (i + 1) * rows, :] = er[i].astype(F32)
    image += dot(xs[...].astype(BF16), proj[0:dv, :])
    img[sec] = image.astype(BF16)
    swap = remote(img.at[sec], img.at[sec], msem.at[0], msem.at[1], section=1 - sec)
    swap_in = remote(img.at[1 - sec], img.at[1 - sec], msem.at[0], msem.at[1], section=1 - sec)
    swap.start()
    pass_cross(tall, ty, tc)
    locals_[4].wait()
    swap_in.wait_recv()

    part_rows = total // G
    image_all = jnp.concatenate([img[0], img[1]], axis=0)

    def head_terms(h):
        k = dot(image_all, kvw[:, pl.ds(pl.multiple_of(h * HD, HD), HD)])
        v = dot(image_all, kvw[:, pl.ds(pl.multiple_of((KV_HEADS + h) * HD, HD), HD)])
        for r in range(G):
            at = slice(r * part_rows, (r + 1) * part_rows)
            kvp[r % 2, h * (G // 2) + r // 2, :, 0:HD] = k[at]
            kvp[r % 2, h * (G // 2) + r // 2, :, HD : 2 * HD] = v[at]

    each(0, KV_HEADS, head_terms)
    kv_pair = remote(kvp.at[1 - c], kcr, kc.at[0], kc.at[1], tensor=pair)
    kv_pair.start()

    each(0, J, lambda j: core_in(tall, tc, j).wait_recv())
    locals_[5].wait()
    query[...] = jnp.zeros_like(query)

    def query_term(b):
        query[...] += dot(tall[b], qw[pl.ds(pl.multiple_of(b * width, width), width), :])

    kv_pair.wait_recv()

    def kv_out(p):
        j = (mj + p) % J
        return remote(kvp.at[c, j], kzr.at[mj], kz.at[0, p], kz.at[1, mj], tensor=j * 2 + c)

    def kv_in(p):
        j = (mj + p) % J
        return remote(kvp.at[c, j], kzr.at[j], kz.at[0, p], kz.at[1, j], tensor=j * 2 + c)

    def kv_send(p):
        j = (mj + p) % J
        kvp[c, j] = kvp[c, j] + kcr[j]
        kv_out(p).start()

    each(1, J, kv_send)
    each(0, T, query_term)
    each(1, J, lambda p: kv_in(p).wait_recv())
    kv_own = lax.fori_loop(
        1, J, lambda p, acc: acc + kzr[(mj + p) % J], kvp[c, mj] + kcr[mj]
    )
    place = me % G
    kvh[place] = kv_own.astype(BF16)

    def share(p):
        to = (me // G) * G + (place + p) % G
        return remote(kvh.at[place], kvh.at[place], kg.at[0, p], kg.at[1, place], tensor=to)

    def share_in(p):
        r = (place + p) % G
        return remote(kvh.at[r], kvh.at[r], kg.at[0, p], kg.at[1, r], tensor=(me // G) * G + r)

    each(1, G, lambda p: share(p).start())
    for h in range(hl):
        q = query[:, h * HD : (h + 1) * HD]
        query[:, h * HD : (h + 1) * HD] = rms_scale(q, qgain[...])
    each(1, G, lambda p: share_in(p).wait_recv())

    kv_all = jnp.concatenate([kvh[r] for r in range(G)], axis=0)
    keys = rms_scale(kv_all[:, 0:HD].astype(F32), kgain[...]).astype(BF16)
    values = kv_all[:, HD : 2 * HD]
    for h in range(hl):
        q = query[:, h * HD : (h + 1) * HD].astype(BF16)
        scores = lax.dot_general(
            q, keys, (((1,), (1,)), ((), ())), preferred_element_type=F32
        ) * (1.0 / HD**0.5)
        scores = jnp.where(mask[...] > 0.5, scores, -1e30)
        weights = jnp.exp(scores - jnp.max(scores, axis=-1, keepdims=True))
        probs = (weights / jnp.sum(weights, axis=-1, keepdims=True)).astype(BF16)
        att[:, h * HD : (h + 1) * HD] = dot(probs, values).astype(BF16)

    locals_[6].wait()

    def columns(zs, yy, cc):
        first = pl.multiple_of(((zs * 2 + yy) * 2 + cc) * width, width)
        return dot(att[...], ow[:, pl.ds(first, width)])

    def pair_out(k):
        return remote(ocs.at[k], ocr.at[k], oc.at[0, k], oc.at[1, k], tensor=pair)

    def across_out(k):
        return remote(oys.at[k], oyr.at[k], oy.at[0, k], oy.at[1, k], tensor=across)

    def line_out(k):
        zs = (z + 1 + k) % A
        return remote(
            ozs.at[k], ozr.at[k], oz.at[0, k], oz.at[1, k], tensor=zs * 4 + y * 2 + c
        )

    def terms_pair(k):
        zs = (z + 1 + k) % A
        for yy in range(2):
            ocs[k, yy] = columns(zs, yy, 1 - c)
        pair_out(k).start()

    def terms_own(k):
        zs = (z + 1 + k) % A
        for yy in range(2):
            own[k, yy] = columns(zs, yy, c)
        pair_out(k).wait_recv()
        oys[k] = (own[k, 1 - y] + ocr[k, 1 - y]).astype(BF16)
        across_out(k).start()

    each(0, A, terms_pair)
    each(0, A, terms_own)

    def terms_line(k):
        across_out(k).wait_recv()
        ozs[k] = (own[k, y] + ocr[k, y] + oyr[k].astype(F32)).astype(BF16)
        line_out(k).start()

    each(0, A - 1, terms_line)
    across_out(A - 1).wait_recv()
    branch = own[A - 1, y] + ocr[A - 1, y] + oyr[A - 1].astype(F32)
    each(0, A - 1, lambda k: line_out(k).wait_recv())
    for k in range(A - 1):
        branch += ozr[k].astype(F32)
    out[...] = (tall[me].astype(F32) + jnp.tanh(gate[...]) * branch).astype(BF16)

    def sent_all(p):
        spread(xr, xsem, p).wait_send()
        part_out(p).wait_send()
        spread(er, esem, p).wait_send()

    each(1, T, sent_all)

    def sent_line(p):
        line(ir, iz, p).wait_send()
        line(tall, tz, p).wait_send()
        line_out(p - 1).wait_send()

    each(1, A, sent_line)

    def sent_cross(zs):
        cross(ir, iy, zs).wait_send()
        cross(tall, ty, zs).wait_send()
        pair_out(zs).wait_send()
        across_out(zs).wait_send()

    each(0, A, sent_cross)

    def sent_core(j):
        core(ir, ic, j).wait_send()
        core(tall, tc, j).wait_send()

    each(0, J, sent_core)
    swap.wait_send()
    kv_pair.wait_send()
    each(1, J, lambda p: kv_out(p).wait_send())
    each(1, G, lambda p: share(p).wait_send())


def shards(T, *arrays):
    (
        patches,
        intermediate,
        fc1_weight,
        fc2_weight,
        projector,
        text,
        query_weight,
        kv_weight,
        query_gain,
        key_gain,
        out_weight,
        attn_gate,
        tile_list,
        list_count,
    ) = arrays
    A, J, G = T // 4, T // 2, T // KV_HEADS
    rows, dv = patches.shape
    inter_w = intermediate.shape[1]
    group = rows * T
    total = group * 2
    _, txt, width = text.shape
    vm = pltpu.VMEM
    pairs = lambda n: pltpu.SemaphoreType.DMA((2, n))
    scratch = [
        vm(fc1_weight.shape, BF16),
        vm(fc2_weight.shape, BF16),
        vm(projector.shape, BF16),
        vm(query_weight.shape[1:], BF16),
        vm(kv_weight.shape[1:], BF16),
        vm(out_weight.shape[1:], BF16),
        vm((T, rows, dv), BF16),
        vm((group, dv), F32),
        vm((T, rows, dv), F32),
        vm((T, rows, dv), F32),
        vm((T, rows, dv), BF16),
        vm((T, rows, inter_w), BF16),
        vm((group, inter_w), F32),
        vm((2, group, width), BF16),
        vm((T, txt, width), BF16),
        vm((txt, width), F32),
        vm((2, J, total // G, 2 * HD), F32),
        vm((J, total // G, 2 * HD), F32),
        vm((J, total // G, 2 * HD), F32),
        vm((G, total // G, 2 * HD), BF16),
        vm((txt, total), F32),
        vm((txt, width), BF16),
        vm((A, 2, txt, width), F32),
        vm((A, 2, txt, width), F32),
        vm((A, 2, txt, width), F32),
        vm((A, txt, width), BF16),
        vm((A, txt, width), BF16),
        vm((A - 1, txt, width), BF16),
        vm((A - 1, txt, width), BF16),
        pltpu.SemaphoreType.DMA((7,)),
        pairs(T),
        pairs(T),
        pairs(T),
        pairs(A),
        pairs(A),
        pairs(J),
        pairs(A),
        pairs(A),
        pairs(J),
        pltpu.SemaphoreType.DMA((2,)),
        pltpu.SemaphoreType.DMA((2,)),
        pairs(J),
        pairs(G),
        pairs(A),
        pairs(A),
        pairs(A),
    ]
    mixed = pl.pallas_call(
        functools.partial(kernel, T),
        out_shape=jax.ShapeDtypeStruct((txt, width), BF16),
        in_specs=[pl.BlockSpec(memory_space=pltpu.VMEM)] * 7
        + [pl.BlockSpec(memory_space=pl.ANY)] * 7,
        out_specs=pl.BlockSpec(memory_space=pltpu.VMEM),
        scratch_shapes=scratch,
        compiler_params=pltpu.CompilerParams(
            collective_id=0, has_side_effects=True, vmem_limit_bytes=60 * 1024 * 1024
        ),
        name="tail",
    )(
        patches,
        intermediate,
        query_gain,
        key_gain,
        attn_gate.reshape(1, 1),
        tile_list[0],
        list_count.reshape(-1, 1),
        text[0],
        fc1_weight,
        fc2_weight,
        projector,
        query_weight[0],
        kv_weight[0],
        out_weight[0],
    )
    return mixed[None]


def solution(mesh):
    placed = (
        P(("section", "tensor"), None),
        P(("section", "tensor"), None),
        P(None, "tensor"),
        P("tensor", None),
        P(None, "tensor"),
        P("section", None, "tensor"),
        P("section", None, "tensor"),
        P("section", "tensor", None),
        P("section", None),
        P("section", None),
        P("section", "tensor", None),
        P("section"),
        P("section", None, None),
        P("section", None),
    )
    return jax.shard_map(
        functools.partial(shards, mesh.shape["tensor"]),
        mesh=mesh,
        in_specs=placed,
        out_specs=P("section", None, "tensor"),
        check_vma=False,
    )
```

```python
import functools

import jax
import jax.numpy as jnp
from jax import lax
from jax.experimental import pallas as pl
from jax.experimental.pallas import tpu as pltpu
from jax.sharding import PartitionSpec as P

HEADS = 64
KV_HEADS = 8
HD = 128
TILE_ROWS = 64
TBLOCK = 64
CHUNKS = 4
F32 = jnp.float32
BF16 = jnp.bfloat16


def dot(a, b):
    return jnp.dot(a, b, preferred_element_type=F32)


def remote(src, dst, send, recv, **axes):
    return pltpu.make_async_remote_copy(
        src_ref=src,
        dst_ref=dst,
        send_sem=send,
        recv_sem=recv,
        device_id=axes,
        device_id_type=pl.DeviceIdType.MESH,
    )


def rms_scale(values, gain):
    return values * lax.rsqrt(jnp.mean(values * values, axis=-1, keepdims=True) + 1e-05) * gain


def each(first, last, body):
    def step(i, carry):
        body(i)
        return carry

    lax.fori_loop(first, last, step, 0)


def kernel(
    T,
    patches,
    inter,
    qgain,
    kgain,
    gate,
    tiles,
    counts,
    text,
    fc1_hbm,
    fc2_hbm,
    proj_hbm,
    qw_hbm,
    kvw_hbm,
    ow_hbm,
    out,
    fc1,
    fc2,
    proj,
    qw,
    kvw,
    ow,
    xr,
    xs,
    part,
    partr,
    er,
    ir,
    feats,
    img,
    tall,
    query,
    kvp,
    kcr,
    kzr,
    kvh,
    mask,
    att,
    ocs,
    ocr,
    own,
    oys,
    oyr,
    ozs,
    ozr,
    loc,
    xsem,
    rsem,
    esem,
    tz,
    ty,
    tc,
    iz,
    iy,
    ic,
    msem,
    kc,
    kz,
    kg,
    oc,
    oy,
    oz,
):
    A = T // 4
    J = T // 2
    G = T // KV_HEADS
    me = lax.axis_index("tensor")
    sec = lax.axis_index("section")
    z = me // 4
    y = (me // 2) % 2
    c = me % 2
    mj = me // 2
    pair = me + 1 - 2 * c
    across = me + 2 - 4 * y
    rows = patches.shape[0]
    group = T * rows
    dv = patches.shape[1]
    txt = tall.shape[1]
    width = tall.shape[2]
    hl = width // HD

    barrier = pltpu.get_barrier_semaphore()

    def greet(p):
        pl.semaphore_signal(
            barrier,
            inc=1,
            device_id={"tensor": (me + p) % T},
            device_id_type=pl.DeviceIdType.MESH,
        )

    each(1, T, greet)
    pl.semaphore_signal(
        barrier, inc=1, device_id={"section": 1 - sec}, device_id_type=pl.DeviceIdType.MESH
    )
    locals_ = [
        pltpu.make_async_copy(src, dst, loc.at[i])
        for i, (src, dst) in enumerate(
            (
                (text, tall.at[me]),
                (fc1_hbm, fc1),
                (fc2_hbm, fc2),
                (proj_hbm, proj),
                (kvw_hbm, kvw),
                (qw_hbm, qw),
                (ow_hbm, ow),
            )
        )
    ]
    for copy in locals_:
        copy.start()
    xr[me] = patches[...]
    ir[me] = inter[...]
    pl.semaphore_wait(barrier, T)

    def spread(buf, sem, p):
        return remote(
            buf.at[me], buf.at[me], sem.at[0, p], sem.at[1, me], tensor=(me + p) % T
        )

    def spread_in(buf, sem, p):
        src = (me + p) % T
        return remote(buf.at[src], buf.at[src], sem.at[0, p], sem.at[1, src], tensor=src)

    def part_out(p):
        to = (me + p) % T
        return remote(part.at[to], partr.at[me], rsem.at[0, p], rsem.at[1, me], tensor=to)

    def part_in(p):
        src = (me + p) % T
        return remote(part.at[src], partr.at[src], rsem.at[0, p], rsem.at[1, src], tensor=src)

    def line(buf, sem, p):
        to = ((z + p) % A) * 4 + y * 2 + c
        return remote(buf.at[me], buf.at[me], sem.at[0, p], sem.at[1, z], tensor=to)

    def line_in(buf, sem, p):
        zs = (z + p) % A
        src = zs * 4 + y * 2 + c
        return remote(buf.at[src], buf.at[src], sem.at[0, p], sem.at[1, zs], tensor=src)

    def cross(buf, sem, zs):
        b = zs * 4 + y * 2 + c
        return remote(buf.at[b], buf.at[b], sem.at[0, zs], sem.at[1, zs], tensor=across)

    def cross_in(buf, sem, zs):
        b = zs * 4 + (1 - y) * 2 + c
        return remote(buf.at[b], buf.at[b], sem.at[0, zs], sem.at[1, zs], tensor=across)

    def core(buf, sem, j):
        b = j * 2 + c
        return remote(buf.at[b], buf.at[b], sem.at[0, j], sem.at[1, j], tensor=pair)

    def core_in(buf, sem, j):
        b = j * 2 + 1 - c
        return remote(buf.at[b], buf.at[b], sem.at[0, j], sem.at[1, j], tensor=pair)

    def begin(buf, lz, ly, lc):
        each(1, A, lambda p: line(buf, lz, p).start())
        cross(buf, ly, z).start()
        core(buf, lc, mj).start()

    def pass_line(buf, lz, ly, lc):
        def body(p):
            zs = (z + p) % A
            line_in(buf, lz, p).wait_recv()
            cross(buf, ly, zs).start()
            core(buf, lc, zs * 2 + y).start()

        each(1, A, body)

    def pass_cross(buf, ly, lc):
        def body(p):
            zs = (z + p) % A
            cross_in(buf, ly, zs).wait_recv()
            core(buf, lc, zs * 2 + 1 - y).start()

        each(0, A, body)

    step = txt // CHUNKS

    def text_copy(b, ch, sem, send, recv, to):
        rows_of = tall.at[b, pl.ds(ch * step, step), :]
        return remote(
            rows_of, rows_of, sem.at[0, send * CHUNKS + ch], sem.at[1, recv * CHUNKS + ch], tensor=to
        )

    def text_line(ch, p):
        return text_copy(me, ch, tz, p, z, ((z + p) % A) * 4 + y * 2 + c)

    def text_line_in(ch, p):
        zs = (z + p) % A
        src = zs * 4 + y * 2 + c
        return text_copy(src, ch, tz, p, zs, src)

    def text_cross(ch, zs):
        return text_copy(zs * 4 + y * 2 + c, ch, ty, zs, zs, across)

    def text_cross_in(ch, zs):
        return text_copy(zs * 4 + (1 - y) * 2 + c, ch, ty, zs, zs, across)

    def text_core(ch, j):
        return text_copy(j * 2 + c, ch, tc, j, j, pair)

    def text_core_in(ch, j):
        return text_copy(j * 2 + 1 - c, ch, tc, j, j, pair)

    def text_begin(ch):
        each(1, A, lambda p: text_line(ch, p).start())
        text_cross(ch, z).start()
        text_core(ch, mj).start()

    def text_pass_line(ch):
        def body(p):
            zs = (z + p) % A
            text_line_in(ch, p).wait_recv()
            text_cross(ch, zs).start()
            text_core(ch, zs * 2 + y).start()

        each(1, A, body)

    def text_pass_cross(ch):
        def body(p):
            zs = (z + p) % A
            text_cross_in(ch, zs).wait_recv()
            text_core(ch, zs * 2 + 1 - y).start()

        each(0, A, body)

    each(1, T, lambda p: spread(xr, xsem, p).start())
    begin(ir, iz, iy, ic)
    locals_[0].wait()
    text_begin(0)

    total = mask.shape[1]
    tile_of = lax.broadcasted_iota(jnp.int32, (TBLOCK, total), 1) // TILE_ROWS
    for b in range(tiles.shape[0]):
        seen = jnp.zeros((TBLOCK, total), F32)
        for j in range(tiles.shape[1]):
            listed = (tile_of == tiles[b : b + 1, j : j + 1]) & (counts[:, b : b + 1] > j)
            seen = jnp.where(listed, 1.0, seen)
        mask[b * TBLOCK : (b + 1) * TBLOCK, :] = seen

    each(1, T, lambda p: spread_in(xr, xsem, p).wait_recv())
    for i in range(T):
        xs[i * rows : (i + 1) * rows, :] = xr[i].astype(F32)
    states = xs[...]
    center = states - jnp.mean(states, axis=-1, keepdims=True)
    spread_sq = jnp.mean(center * center, axis=-1, keepdims=True)
    normed = (center * lax.rsqrt(spread_sq + 1e-06)).astype(BF16)
    locals_[1].wait()
    pre = lax.dot_general(
        normed, fc1[...], (((1,), (1,)), ((), ())), preferred_element_type=F32
    )
    hidden = (0.5 * pre * (1.0 + lax.erf(pre * (0.5**0.5)))).astype(BF16)
    locals_[2].wait()
    partial_value = dot(hidden, fc2[...])
    for i in range(T):
        part[i] = partial_value[i * rows : (i + 1) * rows, :]
    each(1, T, lambda p: part_out(p).start())
    text_begin(1)
    text_pass_line(0)
    pass_line(ir, iz, iy, ic)
    each(1, T, lambda p: part_in(p).wait_recv())
    total_value = lax.fori_loop(
        1, T, lambda p, acc: acc + partr[(me + p) % T], part[me]
    )
    er[me] = (patches[...].astype(F32) + total_value).astype(BF16)
    each(1, T, lambda p: spread(er, esem, p).start())
    text_begin(2)
    text_pass_line(1)
    pass_cross(ir, iy, ic)

    each(0, J, lambda j: core_in(ir, ic, j).wait_recv())
    for i in range(T):
        xs[i * rows : (i + 1) * rows, :] = xr[i].astype(F32)
        feats[i * rows : (i + 1) * rows, :] = ir[i].astype(F32)
    locals_[3].wait()
    image = jnp.zeros((group, width), F32)
    chunks = inter.shape[1] // dv
    for k in range(chunks):
        image += dot(
            feats[:, k * dv : (k + 1) * dv].astype(BF16), proj[(k + 1) * dv : (k + 2) * dv, :]
        )
    each(1, T, lambda p: spread_in(er, esem, p).wait_recv())
    for i in range(T):
        xs[i * rows : (i + 1) * rows, :] = er[i].astype(F32)
    image += dot(xs[...].astype(BF16), proj[0:dv, :])
    img[sec] = image.astype(BF16)
    swap = remote(img.at[sec], img.at[sec], msem.at[0], msem.at[1], section=1 - sec)
    swap_in = remote(img.at[1 - sec], img.at[1 - sec], msem.at[0], msem.at[1], section=1 - sec)
    swap.start()
    text_begin(3)
    text_pass_line(2)
    text_pass_cross(0)
    locals_[4].wait()
    swap_in.wait_recv()

    part_rows = total // G
    image_all = jnp.concatenate([img[0], img[1]], axis=0)

    def head_terms(h):
        k = dot(image_all, kvw[:, pl.ds(pl.multiple_of(h * HD, HD), HD)])
        v = dot(image_all, kvw[:, pl.ds(pl.multiple_of((KV_HEADS + h) * HD, HD), HD)])
        for r in range(G):
            at = slice(r * part_rows, (r + 1) * part_rows)
            kvp[r % 2, h * (G // 2) + r // 2, :, 0:HD] = k[at]
            kvp[r % 2, h * (G // 2) + r // 2, :, HD : 2 * HD] = v[at]

    each(0, KV_HEADS, head_terms)
    kv_pair = remote(kvp.at[1 - c], kcr, kc.at[0], kc.at[1], tensor=pair)
    kv_pair.start()

    text_pass_line(3)
    text_pass_cross(1)


    def query_term(b):
        query[...] += dot(tall[b], qw[pl.ds(pl.multiple_of(b * width, width), width), :])

    kv_pair.wait_recv()

    def kv_out(p):
        j = (mj + p) % J
        return remote(kvp.at[c, j], kzr.at[mj], kz.at[0, p], kz.at[1, mj], tensor=j * 2 + c)

    def kv_in(p):
        j = (mj + p) % J
        return remote(kvp.at[c, j], kzr.at[j], kz.at[0, p], kz.at[1, j], tensor=j * 2 + c)

    def kv_send(p):
        j = (mj + p) % J
        kvp[c, j] = kvp[c, j] + kcr[j]
        kv_out(p).start()

    each(1, J, kv_send)
    for ch in range(2, CHUNKS):
        text_pass_cross(ch)
    for ch in range(CHUNKS):
        each(0, J, lambda j, ch=ch: text_core_in(ch, j).wait_recv())
    locals_[5].wait()
    query[...] = jnp.zeros_like(query)
    each(0, T, query_term)
    each(1, J, lambda p: kv_in(p).wait_recv())
    kv_own = lax.fori_loop(
        1, J, lambda p, acc: acc + kzr[(mj + p) % J], kvp[c, mj] + kcr[mj]
    )
    place = me % G
    kvh[place] = kv_own.astype(BF16)

    def share(p):
        to = (me // G) * G + (place + p) % G
        return remote(kvh.at[place], kvh.at[place], kg.at[0, p], kg.at[1, place], tensor=to)

    def share_in(p):
        r = (place + p) % G
        return remote(kvh.at[r], kvh.at[r], kg.at[0, p], kg.at[1, r], tensor=(me // G) * G + r)

    each(1, G, lambda p: share(p).start())
    for h in range(hl):
        q = query[:, h * HD : (h + 1) * HD]
        query[:, h * HD : (h + 1) * HD] = rms_scale(q, qgain[...])
    each(1, G, lambda p: share_in(p).wait_recv())

    kv_all = jnp.concatenate([kvh[r] for r in range(G)], axis=0)
    keys = rms_scale(kv_all[:, 0:HD].astype(F32), kgain[...]).astype(BF16)
    values = kv_all[:, HD : 2 * HD]
    for h in range(hl):
        q = query[:, h * HD : (h + 1) * HD].astype(BF16)
        scores = lax.dot_general(
            q, keys, (((1,), (1,)), ((), ())), preferred_element_type=F32
        ) * (1.0 / HD**0.5)
        scores = jnp.where(mask[...] > 0.5, scores, -1e30)
        weights = jnp.exp(scores - jnp.max(scores, axis=-1, keepdims=True))
        probs = (weights / jnp.sum(weights, axis=-1, keepdims=True)).astype(BF16)
        att[:, h * HD : (h + 1) * HD] = dot(probs, values).astype(BF16)

    locals_[6].wait()

    def columns(zs, yy, cc):
        first = pl.multiple_of(((zs * 2 + yy) * 2 + cc) * width, width)
        return dot(att[...], ow[:, pl.ds(first, width)])

    def pair_out(k):
        return remote(ocs.at[k], ocr.at[k], oc.at[0, k], oc.at[1, k], tensor=pair)

    def across_out(k):
        return remote(oys.at[k], oyr.at[k], oy.at[0, k], oy.at[1, k], tensor=across)

    def line_out(k):
        zs = (z + 1 + k) % A
        return remote(
            ozs.at[k], ozr.at[k], oz.at[0, k], oz.at[1, k], tensor=zs * 4 + y * 2 + c
        )

    def terms_pair(k):
        zs = (z + 1 + k) % A
        for yy in range(2):
            ocs[k, yy] = columns(zs, yy, 1 - c)
        pair_out(k).start()

    def terms_own(k):
        zs = (z + 1 + k) % A
        for yy in range(2):
            own[k, yy] = columns(zs, yy, c)
        pair_out(k).wait_recv()
        oys[k] = (own[k, 1 - y] + ocr[k, 1 - y]).astype(BF16)
        across_out(k).start()

    each(0, A, terms_pair)
    each(0, A, terms_own)

    def terms_line(k):
        across_out(k).wait_recv()
        ozs[k] = (own[k, y] + ocr[k, y] + oyr[k].astype(F32)).astype(BF16)
        line_out(k).start()

    each(0, A - 1, terms_line)
    across_out(A - 1).wait_recv()
    branch = own[A - 1, y] + ocr[A - 1, y] + oyr[A - 1].astype(F32)
    each(0, A - 1, lambda k: line_out(k).wait_recv())
    for k in range(A - 1):
        branch += ozr[k].astype(F32)
    out[...] = (tall[me].astype(F32) + jnp.tanh(gate[...]) * branch).astype(BF16)

    def sent_all(p):
        spread(xr, xsem, p).wait_send()
        part_out(p).wait_send()
        spread(er, esem, p).wait_send()

    each(1, T, sent_all)

    def sent_line(p):
        line(ir, iz, p).wait_send()
        for ch in range(CHUNKS):
            text_line(ch, p).wait_send()
        line_out(p - 1).wait_send()

    each(1, A, sent_line)

    def sent_cross(zs):
        cross(ir, iy, zs).wait_send()
        for ch in range(CHUNKS):
            text_cross(ch, zs).wait_send()
        pair_out(zs).wait_send()
        across_out(zs).wait_send()

    each(0, A, sent_cross)

    def sent_core(j):
        core(ir, ic, j).wait_send()
        for ch in range(CHUNKS):
            text_core(ch, j).wait_send()

    each(0, J, sent_core)
    swap.wait_send()
    kv_pair.wait_send()
    each(1, J, lambda p: kv_out(p).wait_send())
    each(1, G, lambda p: share(p).wait_send())


def shards(T, *arrays):
    (
        patches,
        intermediate,
        fc1_weight,
        fc2_weight,
        projector,
        text,
        query_weight,
        kv_weight,
        query_gain,
        key_gain,
        out_weight,
        attn_gate,
        tile_list,
        list_count,
    ) = arrays
    A, J, G = T // 4, T // 2, T // KV_HEADS
    rows, dv = patches.shape
    inter_w = intermediate.shape[1]
    group = rows * T
    total = group * 2
    _, txt, width = text.shape
    vm = pltpu.VMEM
    pairs = lambda n: pltpu.SemaphoreType.DMA((2, n))
    scratch = [
        vm(fc1_weight.shape[::-1], BF16),
        vm(fc2_weight.shape, BF16),
        vm(projector.shape, BF16),
        vm(query_weight.shape[1:], BF16),
        vm(kv_weight.shape[1:], BF16),
        vm(out_weight.shape[1:], BF16),
        vm((T, rows, dv), BF16),
        vm((group, dv), F32),
        vm((T, rows, dv), F32),
        vm((T, rows, dv), F32),
        vm((T, rows, dv), BF16),
        vm((T, rows, inter_w), BF16),
        vm((group, inter_w), F32),
        vm((2, group, width), BF16),
        vm((T, txt, width), BF16),
        vm((txt, width), F32),
        vm((2, J, total // G, 2 * HD), F32),
        vm((J, total // G, 2 * HD), F32),
        vm((J, total // G, 2 * HD), F32),
        vm((G, total // G, 2 * HD), BF16),
        vm((txt, total), F32),
        vm((txt, width), BF16),
        vm((A, 2, txt, width), F32),
        vm((A, 2, txt, width), F32),
        vm((A, 2, txt, width), F32),
        vm((A, txt, width), BF16),
        vm((A, txt, width), BF16),
        vm((A - 1, txt, width), BF16),
        vm((A - 1, txt, width), BF16),
        pltpu.SemaphoreType.DMA((7,)),
        pairs(T),
        pairs(T),
        pairs(T),
        pairs(A * CHUNKS),
        pairs(A * CHUNKS),
        pairs(J * CHUNKS),
        pairs(A),
        pairs(A),
        pairs(J),
        pltpu.SemaphoreType.DMA((2,)),
        pltpu.SemaphoreType.DMA((2,)),
        pairs(J),
        pairs(G),
        pairs(A),
        pairs(A),
        pairs(A),
    ]
    mixed = pl.pallas_call(
        functools.partial(kernel, T),
        out_shape=jax.ShapeDtypeStruct((txt, width), BF16),
        in_specs=[pl.BlockSpec(memory_space=pltpu.VMEM)] * 7
        + [pl.BlockSpec(memory_space=pl.ANY)] * 7,
        out_specs=pl.BlockSpec(memory_space=pltpu.VMEM),
        scratch_shapes=scratch,
        compiler_params=pltpu.CompilerParams(
            collective_id=0, has_side_effects=True, vmem_limit_bytes=60 * 1024 * 1024
        ),
        name="tail",
    )(
        patches,
        intermediate,
        query_gain,
        key_gain,
        attn_gate.reshape(1, 1),
        tile_list[0],
        list_count,
        text[0],
        fc1_weight.T,
        fc2_weight,
        projector,
        query_weight[0],
        kv_weight[0],
        out_weight[0],
    )
    return mixed[None]


def solution(mesh):
    placed = (
        P(("section", "tensor"), None),
        P(("section", "tensor"), None),
        P(None, "tensor"),
        P("tensor", None),
        P(None, "tensor"),
        P("section", None, "tensor"),
        P("section", None, "tensor"),
        P("section", "tensor", None),
        P("section", None),
        P("section", None),
        P("section", "tensor", None),
        P("section"),
        P("section", None, None),
        P("section", None),
    )
    return jax.shard_map(
        functools.partial(shards, mesh.shape["tensor"]),
        mesh=mesh,
        in_specs=placed,
        out_specs=P("section", None, "tensor"),
        check_vma=False,
    )
```

```python
import functools

import jax
import jax.numpy as jnp
from jax import lax
from jax.experimental import pallas as pl
from jax.experimental.pallas import tpu as pltpu
from jax.sharding import PartitionSpec as P

HEADS = 64
KV_HEADS = 8
HD = 128
TILE_ROWS = 64
TBLOCK = 64
CHUNKS = 4
CUTS = 2
LAG = 3
F32 = jnp.float32
BF16 = jnp.bfloat16


def dot(a, b):
    return jnp.dot(a, b, preferred_element_type=F32)


def remote(src, dst, send, recv, **axes):
    return pltpu.make_async_remote_copy(
        src_ref=src,
        dst_ref=dst,
        send_sem=send,
        recv_sem=recv,
        device_id=axes,
        device_id_type=pl.DeviceIdType.MESH,
    )


def rms_scale(values, gain):
    return values * lax.rsqrt(jnp.mean(values * values, axis=-1, keepdims=True) + 1e-05) * gain


def each(first, last, body):
    def step(i, carry):
        body(i)
        return carry

    lax.fori_loop(first, last, step, 0)


def kernel(
    T,
    patches,
    inter,
    qgain,
    kgain,
    gate,
    tiles,
    counts,
    text,
    fc1_hbm,
    fc2_hbm,
    proj_hbm,
    qw_hbm,
    kvw_hbm,
    ow_hbm,
    out,
    fc1,
    fc2,
    proj,
    qw,
    kvw,
    ow,
    xr,
    xs,
    part,
    partr,
    er,
    ir,
    feats,
    img,
    tall,
    query,
    kvp,
    kcr,
    kzr,
    kvh,
    mask,
    att,
    ocs,
    ocr,
    own,
    oys,
    oyr,
    ozs,
    ozr,
    loc,
    xsem,
    rsem,
    esem,
    tz,
    ty,
    tc,
    iz,
    iy,
    ic,
    msem,
    kc,
    kz,
    kg,
    oc,
    oy,
    oz,
):
    A = T // 4
    J = T // 2
    G = T // KV_HEADS
    me = lax.axis_index("tensor")
    sec = lax.axis_index("section")
    z = me // 4
    y = (me // 2) % 2
    c = me % 2
    mj = me // 2
    pair = me + 1 - 2 * c
    across = me + 2 - 4 * y
    rows = patches.shape[0]
    group = T * rows
    dv = patches.shape[1]
    txt = tall.shape[1]
    width = tall.shape[2]
    hl = width // HD

    barrier = pltpu.get_barrier_semaphore()

    def greet(p):
        pl.semaphore_signal(
            barrier,
            inc=1,
            device_id={"tensor": (me + p) % T},
            device_id_type=pl.DeviceIdType.MESH,
        )

    each(1, T, greet)
    pl.semaphore_signal(
        barrier, inc=1, device_id={"section": 1 - sec}, device_id_type=pl.DeviceIdType.MESH
    )
    locals_ = [
        pltpu.make_async_copy(src, dst, loc.at[i])
        for i, (src, dst) in enumerate(
            (
                (text, tall.at[me]),
                (fc1_hbm, fc1),
                (fc2_hbm, fc2),
                (proj_hbm, proj),
                (kvw_hbm, kvw),
                (qw_hbm, qw),
                (ow_hbm, ow),
            )
        )
    ]
    for copy in locals_:
        copy.start()
    xr[me] = patches[...]
    ir[me] = inter[...]
    pl.semaphore_wait(barrier, T)

    def spread(buf, sem, p):
        return remote(
            buf.at[me], buf.at[me], sem.at[0, p], sem.at[1, me], tensor=(me + p) % T
        )

    def spread_in(buf, sem, p):
        src = (me + p) % T
        return remote(buf.at[src], buf.at[src], sem.at[0, p], sem.at[1, src], tensor=src)

    def part_out(p):
        to = (me + p) % T
        return remote(part.at[to], partr.at[me], rsem.at[0, p], rsem.at[1, me], tensor=to)

    def part_in(p):
        src = (me + p) % T
        return remote(part.at[src], partr.at[src], rsem.at[0, p], rsem.at[1, src], tensor=src)

    def line(buf, sem, p):
        to = ((z + p) % A) * 4 + y * 2 + c
        return remote(buf.at[me], buf.at[me], sem.at[0, p], sem.at[1, z], tensor=to)

    def line_in(buf, sem, p):
        zs = (z + p) % A
        src = zs * 4 + y * 2 + c
        return remote(buf.at[src], buf.at[src], sem.at[0, p], sem.at[1, zs], tensor=src)

    def cross(buf, sem, zs):
        b = zs * 4 + y * 2 + c
        return remote(buf.at[b], buf.at[b], sem.at[0, zs], sem.at[1, zs], tensor=across)

    def cross_in(buf, sem, zs):
        b = zs * 4 + (1 - y) * 2 + c
        return remote(buf.at[b], buf.at[b], sem.at[0, zs], sem.at[1, zs], tensor=across)

    def core(buf, sem, j):
        b = j * 2 + c
        return remote(buf.at[b], buf.at[b], sem.at[0, j], sem.at[1, j], tensor=pair)

    def core_in(buf, sem, j):
        b = j * 2 + 1 - c
        return remote(buf.at[b], buf.at[b], sem.at[0, j], sem.at[1, j], tensor=pair)

    def begin(buf, lz, ly, lc):
        each(1, A, lambda p: line(buf, lz, p).start())
        cross(buf, ly, z).start()
        core(buf, lc, mj).start()

    def pass_line(buf, lz, ly, lc):
        def body(p):
            zs = (z + p) % A
            line_in(buf, lz, p).wait_recv()
            cross(buf, ly, zs).start()
            core(buf, lc, zs * 2 + y).start()

        each(1, A, body)

    def pass_cross(buf, ly, lc):
        def body(p):
            zs = (z + p) % A
            cross_in(buf, ly, zs).wait_recv()
            core(buf, lc, zs * 2 + 1 - y).start()

        each(0, A, body)

    step = txt // CHUNKS

    def text_copy(b, ch, sem, send, recv, to):
        rows_of = tall.at[b, pl.ds(ch * step, step), :]
        return remote(
            rows_of, rows_of, sem.at[0, send * CHUNKS + ch], sem.at[1, recv * CHUNKS + ch], tensor=to
        )

    def text_line(ch, p):
        return text_copy(me, ch, tz, p, z, ((z + p) % A) * 4 + y * 2 + c)

    def text_line_in(ch, p):
        zs = (z + p) % A
        src = zs * 4 + y * 2 + c
        return text_copy(src, ch, tz, p, zs, src)

    def text_cross(ch, zs):
        return text_copy(zs * 4 + y * 2 + c, ch, ty, zs, zs, across)

    def text_cross_in(ch, zs):
        return text_copy(zs * 4 + (1 - y) * 2 + c, ch, ty, zs, zs, across)

    def text_core(ch, j):
        return text_copy(j * 2 + c, ch, tc, j, j, pair)

    def text_core_in(ch, j):
        return text_copy(j * 2 + 1 - c, ch, tc, j, j, pair)

    def text_begin(ch):
        each(1, A, lambda p: text_line(ch, p).start())
        text_cross(ch, z).start()
        text_core(ch, mj).start()

    def text_pass_line(ch):
        def body(p):
            zs = (z + p) % A
            text_line_in(ch, p).wait_recv()
            text_cross(ch, zs).start()
            text_core(ch, zs * 2 + y).start()

        each(1, A, body)

    def text_pass_cross(ch):
        def body(p):
            zs = (z + p) % A
            text_cross_in(ch, zs).wait_recv()
            text_core(ch, zs * 2 + 1 - y).start()

        each(0, A, body)

    each(1, T, lambda p: spread(xr, xsem, p).start())
    begin(ir, iz, iy, ic)
    locals_[0].wait()
    text_begin(0)

    total = mask.shape[1]
    tile_of = lax.broadcasted_iota(jnp.int32, (TBLOCK, total), 1) // TILE_ROWS
    for b in range(tiles.shape[0]):
        seen = jnp.zeros((TBLOCK, total), F32)
        for j in range(tiles.shape[1]):
            listed = (tile_of == tiles[b : b + 1, j : j + 1]) & (counts[:, b : b + 1] > j)
            seen = jnp.where(listed, 1.0, seen)
        mask[b * TBLOCK : (b + 1) * TBLOCK, :] = seen

    each(1, T, lambda p: spread_in(xr, xsem, p).wait_recv())
    for i in range(T):
        xs[i * rows : (i + 1) * rows, :] = xr[i].astype(F32)
    states = xs[...]
    center = states - jnp.mean(states, axis=-1, keepdims=True)
    spread_sq = jnp.mean(center * center, axis=-1, keepdims=True)
    normed = (center * lax.rsqrt(spread_sq + 1e-06)).astype(BF16)
    locals_[1].wait()
    pre = lax.dot_general(
        normed, fc1[...], (((1,), (1,)), ((), ())), preferred_element_type=F32
    )
    hidden = (0.5 * pre * (1.0 + lax.erf(pre * (0.5**0.5)))).astype(BF16)
    locals_[2].wait()
    partial_value = dot(hidden, fc2[...])
    for i in range(T):
        part[i] = partial_value[i * rows : (i + 1) * rows, :]
    each(1, T, lambda p: part_out(p).start())
    text_begin(1)
    text_pass_line(0)
    pass_line(ir, iz, iy, ic)
    each(1, T, lambda p: part_in(p).wait_recv())
    total_value = lax.fori_loop(
        1, T, lambda p, acc: acc + partr[(me + p) % T], part[me]
    )
    er[me] = (patches[...].astype(F32) + total_value).astype(BF16)
    each(1, T, lambda p: spread(er, esem, p).start())
    text_begin(2)
    text_pass_line(1)
    pass_cross(ir, iy, ic)

    each(0, J, lambda j: core_in(ir, ic, j).wait_recv())
    for i in range(T):
        xs[i * rows : (i + 1) * rows, :] = xr[i].astype(F32)
        feats[i * rows : (i + 1) * rows, :] = ir[i].astype(F32)
    locals_[3].wait()
    image = jnp.zeros((group, width), F32)
    chunks = inter.shape[1] // dv
    for k in range(chunks):
        image += dot(
            feats[:, k * dv : (k + 1) * dv].astype(BF16), proj[(k + 1) * dv : (k + 2) * dv, :]
        )
    each(1, T, lambda p: spread_in(er, esem, p).wait_recv())
    for i in range(T):
        xs[i * rows : (i + 1) * rows, :] = er[i].astype(F32)
    image += dot(xs[...].astype(BF16), proj[0:dv, :])
    img[sec] = image.astype(BF16)
    swap = remote(img.at[sec], img.at[sec], msem.at[0], msem.at[1], section=1 - sec)
    swap_in = remote(img.at[1 - sec], img.at[1 - sec], msem.at[0], msem.at[1], section=1 - sec)
    swap.start()
    text_begin(3)
    text_pass_line(2)
    text_pass_cross(0)
    locals_[4].wait()
    swap_in.wait_recv()

    part_rows = total // G
    image_all = jnp.concatenate([img[0], img[1]], axis=0)

    def head_terms(h):
        k = dot(image_all, kvw[:, pl.ds(pl.multiple_of(h * HD, HD), HD)])
        v = dot(image_all, kvw[:, pl.ds(pl.multiple_of((KV_HEADS + h) * HD, HD), HD)])
        for r in range(G):
            at = slice(r * part_rows, (r + 1) * part_rows)
            kvp[r % 2, h * (G // 2) + r // 2, :, 0:HD] = k[at]
            kvp[r % 2, h * (G // 2) + r // 2, :, HD : 2 * HD] = v[at]

    each(0, KV_HEADS, head_terms)
    kv_pair = remote(kvp.at[1 - c], kcr, kc.at[0], kc.at[1], tensor=pair)
    kv_pair.start()

    text_pass_line(3)
    text_pass_cross(1)


    def query_term(b):
        query[...] += dot(tall[b], qw[pl.ds(pl.multiple_of(b * width, width), width), :])

    kv_pair.wait_recv()

    def kv_out(p):
        j = (mj + p) % J
        return remote(kvp.at[c, j], kzr.at[mj], kz.at[0, p], kz.at[1, mj], tensor=j * 2 + c)

    def kv_in(p):
        j = (mj + p) % J
        return remote(kvp.at[c, j], kzr.at[j], kz.at[0, p], kz.at[1, j], tensor=j * 2 + c)

    def kv_send(p):
        j = (mj + p) % J
        kvp[c, j] = kvp[c, j] + kcr[j]
        kv_out(p).start()

    each(1, J, kv_send)
    for ch in range(2, CHUNKS):
        text_pass_cross(ch)
    for ch in range(CHUNKS):
        each(0, J, lambda j, ch=ch: text_core_in(ch, j).wait_recv())
    locals_[5].wait()
    query[...] = jnp.zeros_like(query)
    each(0, T, query_term)
    each(1, J, lambda p: kv_in(p).wait_recv())
    kv_own = lax.fori_loop(
        1, J, lambda p, acc: acc + kzr[(mj + p) % J], kvp[c, mj] + kcr[mj]
    )
    place = me % G
    kvh[place] = kv_own.astype(BF16)

    def share(p):
        to = (me // G) * G + (place + p) % G
        return remote(kvh.at[place], kvh.at[place], kg.at[0, p], kg.at[1, place], tensor=to)

    def share_in(p):
        r = (place + p) % G
        return remote(kvh.at[r], kvh.at[r], kg.at[0, p], kg.at[1, r], tensor=(me // G) * G + r)

    each(1, G, lambda p: share(p).start())
    for h in range(hl):
        q = query[:, h * HD : (h + 1) * HD]
        query[:, h * HD : (h + 1) * HD] = rms_scale(q, qgain[...])
    each(1, G, lambda p: share_in(p).wait_recv())

    kv_all = jnp.concatenate([kvh[r] for r in range(G)], axis=0)
    keys = rms_scale(kv_all[:, 0:HD].astype(F32), kgain[...]).astype(BF16)
    values = kv_all[:, HD : 2 * HD]
    for h in range(hl):
        q = query[:, h * HD : (h + 1) * HD].astype(BF16)
        scores = lax.dot_general(
            q, keys, (((1,), (1,)), ((), ())), preferred_element_type=F32
        ) * (1.0 / HD**0.5)
        scores = jnp.where(mask[...] > 0.5, scores, -1e30)
        weights = jnp.exp(scores - jnp.max(scores, axis=-1, keepdims=True))
        probs = (weights / jnp.sum(weights, axis=-1, keepdims=True)).astype(BF16)
        att[:, h * HD : (h + 1) * HD] = dot(probs, values).astype(BF16)

    locals_[6].wait()

    S = A * CUTS
    half = txt // CUTS

    def columns(s, yy, cc):
        zs = (z + 1 + s // CUTS) % A
        first = pl.multiple_of(((zs * 2 + yy) * 2 + cc) * width, width)
        at = pl.multiple_of((s % CUTS) * half, half)
        return dot(att[pl.ds(at, half), :], ow[:, pl.ds(first, width)])

    def pair_out(s):
        return remote(ocs.at[s], ocr.at[s], oc.at[0, s], oc.at[1, s], tensor=pair)

    def across_out(s):
        return remote(oys.at[s], oyr.at[s], oy.at[0, s], oy.at[1, s], tensor=across)

    def line_out(s):
        zs = (z + 1 + s // CUTS) % A
        return remote(
            ozs.at[s], ozr.at[s], oz.at[0, s], oz.at[1, s], tensor=zs * 4 + y * 2 + c
        )

    def terms_pair(s):
        for yy in range(2):
            ocs[s, yy] = columns(s, yy, 1 - c)
        pair_out(s).start()

    def terms_own(s):
        for yy in range(2):
            own[s, yy] = columns(s, yy, c)
        pair_out(s).wait_recv()
        oys[s] = (own[s, 1 - y] + ocr[s, 1 - y]).astype(BF16)
        across_out(s).start()

    def terms_both(s):
        terms_pair(s)
        terms_own(s - 1)

    def terms_line(s):
        across_out(s).wait_recv()
        ozs[s] = (own[s, y] + ocr[s, y] + oyr[s].astype(F32)).astype(BF16)
        line_out(s).start()

    def terms_three(s):
        terms_both(s)
        terms_line(s - LAG)

    terms_pair(0)
    each(1, LAG, terms_both)
    each(LAG, S, terms_three)
    terms_own(S - 1)
    each(S - LAG, S - CUTS, terms_line)
    for r in range(CUTS):
        s = S - CUTS + r
        at = slice(r * half, (r + 1) * half)
        across_out(s).wait_recv()
        branch = own[s, y] + ocr[s, y] + oyr[s].astype(F32)
        each(0, A - 1, lambda k, r=r: line_out(k * CUTS + r).wait_recv())
        for k in range(A - 1):
            branch += ozr[k * CUTS + r].astype(F32)
        out[at, :] = (tall[me, at, :].astype(F32) + jnp.tanh(gate[...]) * branch).astype(BF16)

    def sent_all(p):
        spread(xr, xsem, p).wait_send()
        part_out(p).wait_send()
        spread(er, esem, p).wait_send()

    each(1, T, sent_all)

    def sent_line(p):
        line(ir, iz, p).wait_send()
        for ch in range(CHUNKS):
            text_line(ch, p).wait_send()
        for r in range(CUTS):
            line_out((p - 1) * CUTS + r).wait_send()

    each(1, A, sent_line)

    def sent_cross(zs):
        cross(ir, iy, zs).wait_send()
        for ch in range(CHUNKS):
            text_cross(ch, zs).wait_send()
        for r in range(CUTS):
            pair_out(zs * CUTS + r).wait_send()
            across_out(zs * CUTS + r).wait_send()

    each(0, A, sent_cross)

    def sent_core(j):
        core(ir, ic, j).wait_send()
        for ch in range(CHUNKS):
            text_core(ch, j).wait_send()

    each(0, J, sent_core)
    swap.wait_send()
    kv_pair.wait_send()
    each(1, J, lambda p: kv_out(p).wait_send())
    each(1, G, lambda p: share(p).wait_send())


def shards(T, *arrays):
    (
        patches,
        intermediate,
        fc1_weight,
        fc2_weight,
        projector,
        text,
        query_weight,
        kv_weight,
        query_gain,
        key_gain,
        out_weight,
        attn_gate,
        tile_list,
        list_count,
    ) = arrays
    A, J, G = T // 4, T // 2, T // KV_HEADS
    rows, dv = patches.shape
    inter_w = intermediate.shape[1]
    group = rows * T
    total = group * 2
    _, txt, width = text.shape
    vm = pltpu.VMEM
    pairs = lambda n: pltpu.SemaphoreType.DMA((2, n))
    scratch = [
        vm(fc1_weight.shape[::-1], BF16),
        vm(fc2_weight.shape, BF16),
        vm(projector.shape, BF16),
        vm(query_weight.shape[1:], BF16),
        vm(kv_weight.shape[1:], BF16),
        vm(out_weight.shape[1:], BF16),
        vm((T, rows, dv), BF16),
        vm((group, dv), F32),
        vm((T, rows, dv), F32),
        vm((T, rows, dv), F32),
        vm((T, rows, dv), BF16),
        vm((T, rows, inter_w), BF16),
        vm((group, inter_w), F32),
        vm((2, group, width), BF16),
        vm((T, txt, width), BF16),
        vm((txt, width), F32),
        vm((2, J, total // G, 2 * HD), F32),
        vm((J, total // G, 2 * HD), F32),
        vm((J, total // G, 2 * HD), F32),
        vm((G, total // G, 2 * HD), BF16),
        vm((txt, total), F32),
        vm((txt, width), BF16),
        vm((A * CUTS, 2, txt // CUTS, width), F32),
        vm((A * CUTS, 2, txt // CUTS, width), F32),
        vm((A * CUTS, 2, txt // CUTS, width), F32),
        vm((A * CUTS, txt // CUTS, width), BF16),
        vm((A * CUTS, txt // CUTS, width), BF16),
        vm(((A - 1) * CUTS, txt // CUTS, width), BF16),
        vm(((A - 1) * CUTS, txt // CUTS, width), BF16),
        pltpu.SemaphoreType.DMA((7,)),
        pairs(T),
        pairs(T),
        pairs(T),
        pairs(A * CHUNKS),
        pairs(A * CHUNKS),
        pairs(J * CHUNKS),
        pairs(A),
        pairs(A),
        pairs(J),
        pltpu.SemaphoreType.DMA((2,)),
        pltpu.SemaphoreType.DMA((2,)),
        pairs(J),
        pairs(G),
        pairs(A * CUTS),
        pairs(A * CUTS),
        pairs(A * CUTS),
    ]
    mixed = pl.pallas_call(
        functools.partial(kernel, T),
        out_shape=jax.ShapeDtypeStruct((txt, width), BF16),
        in_specs=[pl.BlockSpec(memory_space=pltpu.VMEM)] * 7
        + [pl.BlockSpec(memory_space=pl.ANY)] * 7,
        out_specs=pl.BlockSpec(memory_space=pltpu.VMEM),
        scratch_shapes=scratch,
        compiler_params=pltpu.CompilerParams(
            collective_id=0, has_side_effects=True, vmem_limit_bytes=60 * 1024 * 1024
        ),
        name="tail",
    )(
        patches,
        intermediate,
        query_gain,
        key_gain,
        attn_gate.reshape(1, 1),
        tile_list[0],
        list_count,
        text[0],
        fc1_weight.T,
        fc2_weight,
        projector,
        query_weight[0],
        kv_weight[0],
        out_weight[0],
    )
    return mixed[None]


def solution(mesh):
    placed = (
        P(("section", "tensor"), None),
        P(("section", "tensor"), None),
        P(None, "tensor"),
        P("tensor", None),
        P(None, "tensor"),
        P("section", None, "tensor"),
        P("section", None, "tensor"),
        P("section", "tensor", None),
        P("section", None),
        P("section", None),
        P("section", "tensor", None),
        P("section"),
        P("section", None, None),
        P("section", None),
    )
    return jax.shard_map(
        functools.partial(shards, mesh.shape["tensor"]),
        mesh=mesh,
        in_specs=placed,
        out_specs=P("section", None, "tensor"),
        check_vma=False,
    )
```
